256 devices in a mesh: ctx: 32 (over x, z), cls: 8 (over y, core).
Axes of the slice: x: 4, y: 4, z: 8, core: 2. Of those that a mesh axis runs over, the one named last changes fastest.
Arguments:
- tokens: bfloat16 [196608, 8192], P(('ctx', 'cls')), may hold values from -80 to 80
- doc_length: int32 [1], replicated, may hold values from 98304 to 196608
- queries: bfloat16 [64, 8192], P('cls', 'ctx'), may hold values from -0.046875 to 0.046875
- norm_gain: float32 [8192], P('ctx'), may hold values from 0.1 to 1.9
- head_weight: bfloat16 [8192, 4096], P('ctx', 'cls'), may hold values from -0.0625 to 0.0625
- head_bias: float32 [4096], P('cls'), may hold values from -20 to 20
- labels: int32 [4096], P('cls'), may hold values 0 or 1
Outputs:
- mean_loss: float32 [], replicated
- query_grad: float32 [64, 8192], P('cls', 'ctx')
- head_grad: float32 [8192, 4096], P('ctx', 'cls')
- bias_grad: float32 [4096], P('cls')
The draws below stay inside these ranges and needn't reach their ends.
All inputs are finite; a program needn't handle non-finite values. No bound on the sum of `labels` on one device may be relied on, other than what follows from the above.
Results may differ from the reference program's by a relative error of at most 0.017.
Values may be sent and summed in bfloat16 or wider, within the bound.
A program may use at most 64 MiB of HBM per device.

```python
import math
import jax
import jax.numpy as jnp
from jax import lax

D = 8192
H = 64
A = 4096
AQ = 64
TOKENS = 196608
N_CTX = 32


def draw_tokens(key, part):
    row_key, col_key, noise_key = jax.random.split(jax.random.fold_in(key, 5), 3)
    row_scale = jnp.exp(jax.random.uniform(row_key, (TOKENS, 1), jnp.float32, math.log(0.3), math.log(3.0)))
    col_noise = jnp.exp(jax.random.uniform(col_key, (1, D), jnp.float32, math.log(0.5), math.log(1.5)))
    column_pos = jnp.arange(D, dtype=jnp.float32)[None, :] / D
    col_scale = col_noise * jnp.exp(math.log(3.0) * column_pos)
    base_noise = jnp.clip(jax.random.normal(noise_key, (TOKENS, D), jnp.float32), -5.0, 5.0)
    values = base_noise * row_scale * col_scale
    return values.astype(jnp.bfloat16)


def draw_queries(key, part):
    noise_key = jax.random.fold_in(key, 17)
    spread = 0.25 / math.sqrt(D)
    values = jnp.clip(jax.random.normal(noise_key, (H, D), jnp.float32), -5.0, 5.0) * spread
    return values.astype(jnp.bfloat16)


def draw_head_bias(key, part):
    noise_key = jax.random.fold_in(key, 29)
    position = jnp.arange(A, dtype=jnp.float32) / A
    scale = 0.4 * jnp.exp(math.log(10.0) * position)
    values = jnp.clip(jax.random.normal(noise_key, (A,), jnp.float32), -4.0, 4.0) * scale
    return values.astype(jnp.float32)


def with_ends(values, own_key, smallest, top_value):
    extent = values.shape
    place = [jax.random.randint(jax.random.fold_in(own_key, axis), (), 0, extent[axis]) for axis in range(len(extent))]
    values = values.at[tuple(place)].set(smallest)
    longest = extent.index(max(extent))
    place[longest] = (place[longest] + 1) % extent[longest]
    return values.at[tuple(place)].set(top_value)


def block_scale(rng, dims, shards, smallest, largest):
    level, own = 1.0, jax.random.fold_in(rng, 6)
    for axis_at, blocks in shards:
        draws = jnp.exp(jax.random.uniform(jax.random.fold_in(own, axis_at), (blocks,), jnp.float32, smallest / len(shards), largest / len(shards)))
        level = level * jnp.repeat(draws, dims[axis_at] // blocks).reshape([-1 if axis == axis_at else 1 for axis in range(len(dims))])
    return level


def gaussian(own_key, extent, scale, reach, pieces=(), held_as=jnp.bfloat16):
    entries = scale * jax.random.normal(own_key, extent, jnp.float32)
    if pieces:
        entries = entries * block_scale(own_key, extent, pieces, -0.22, 0.18)
    return jnp.clip(entries, -reach, reach).astype(held_as)


def setup_inputs(seed: int = 0) -> dict:
    arg_keys = jax.random.split(jax.random.key(seed), 8)
    tokens = draw_tokens(jax.random.fold_in(arg_keys[7], 71), 0)
    doc_length = jax.random.randint(arg_keys[1], (1,), TOKENS // 2, TOKENS + 1).astype(jnp.int32)
    queries = draw_queries(jax.random.fold_in(arg_keys[7], 71), 0)
    norm_gain = jnp.clip(1.0 + 0.18 * jax.random.normal(arg_keys[3], (D,), jnp.float32), 0.1, 1.9)
    head_weight = gaussian(arg_keys[4], (D, A), D ** -0.5, 0.0625, ((0, 32), (1, 8)))
    head_bias = draw_head_bias(jax.random.fold_in(arg_keys[7], 71), 0)
    labels = with_ends((jax.random.randint(arg_keys[6], (A,), 0, 2) < 1).astype(jnp.int32), jax.random.fold_in(arg_keys[6], 1), 0, 1)
    return dict(tokens=tokens, doc_length=doc_length, queries=queries, norm_gain=norm_gain, head_weight=head_weight, head_bias=head_bias, labels=labels)


def reference(tokens, doc_length, queries, norm_gain, head_weight, head_bias, labels):
    block_count = N_CTX
    block_rows = TOKENS // block_count
    token_blocks = tokens.reshape(block_count, block_rows, D)

    def score_block(carry, block):
        return (carry, jnp.dot(queries, block.T, preferred_element_type=jnp.float32))
    _, scores = lax.scan(score_block, 0, token_blocks)
    position = (jnp.arange(block_count, dtype=jnp.int32)[:, None] * block_rows + jnp.arange(block_rows, dtype=jnp.int32)[None, :]).astype(jnp.int32)
    valid_mask = (position < doc_length[0])[:, None, :]
    peak = lax.optimization_barrier(jnp.max(jnp.where(valid_mask, scores, -1e+30), axis=(0, 2)))
    weights = jnp.exp(jnp.where(valid_mask, scores - peak[None, :, None], -1e+30))
    weights_b = weights.astype(jnp.bfloat16)

    def pool_block(running, pair):
        return (running + jnp.dot(pair[0], pair[1], preferred_element_type=jnp.float32), 0)
    pooled, _ = lax.scan(pool_block, jnp.zeros((H, D), jnp.float32), (weights_b, token_blocks))
    inverse_rms = lax.rsqrt(lax.optimization_barrier(jnp.sum(pooled * pooled, axis=1)) / D + 1e-05)
    scaled_b = (pooled * norm_gain[None, :]).astype(jnp.bfloat16)
    head_blocks = head_weight.reshape(D, H, AQ).astype(jnp.float32)
    logit_raw = jnp.einsum('hd,dha->ha', scaled_b.astype(jnp.float32), head_blocks, precision=lax.Precision.HIGHEST)
    logits = inverse_rms[:, None] * logit_raw + head_bias.reshape(H, AQ)
    target = labels.reshape(H, AQ).astype(jnp.float32)
    mean_loss = jnp.sum(jax.nn.softplus(logits) - target * logits) / A
    logit_grad = jax.nn.sigmoid(logits) - target
    normed = pooled * inverse_rms[:, None] * norm_gain[None, :]
    head_grad = jnp.einsum('hd,ha->dha', normed, logit_grad, precision=lax.Precision.HIGHEST).reshape(D, A)
    normed_grad = jnp.einsum('dha,ha->hd', head_blocks, logit_grad, precision=lax.Precision.HIGHEST) * norm_gain[None, :]
    unit_pooled = pooled * inverse_rms[:, None]
    inner_mean = lax.optimization_barrier(jnp.sum(unit_pooled * normed_grad, axis=1)) / D
    pooled_grad = (inverse_rms[:, None] * (normed_grad - unit_pooled * inner_mean[:, None])).astype(jnp.bfloat16)

    def grad_block(running, pair):
        projected = jnp.dot(pooled_grad, pair[1].T, preferred_element_type=jnp.float32)
        score_grad = (pair[0] * projected).astype(jnp.bfloat16)
        return (running + jnp.dot(score_grad, pair[1], preferred_element_type=jnp.float32), 0)
    query_grad, _ = lax.scan(grad_block, jnp.zeros((H, D), jnp.float32), (weights, token_blocks))
    return (mean_loss, query_grad, head_grad, logit_grad.reshape(A))
```

```python
import jax
import jax.numpy as jnp
from jax import lax
from jax.experimental import pallas as pl
from jax.experimental.pallas import tpu as pltpu
from jax.sharding import PartitionSpec as P

MESH = pl.DeviceIdType.MESH
F32, BF16 = jnp.float32, jnp.bfloat16
NT = (((1,), (1,)), ((), ()))
TN = (((0,), (0,)), ((), ()))
SIDE, DEPTH = 4, 8
SPAN = 2048
FAR = -1e30
ORDER = (2, 1, 3, 0)


def kernel(
    doc_ref, tokens_hbm, query_ref, gain_ref, head_hbm, bias_ref, label_ref,
    loss_ref, query_grad_ref, head_grad_hbm, bias_grad_ref,
    tok, head, head_grad, gathered1, gathered2, rhs, scores, weights, lhs, total,
    pair_send1, pair_recv1, a_send1, a_recv1, b_send1, b_recv1,
    pair_send2, pair_recv2, a_send2, a_recv2, b_send2, b_recv2,
    peak_own, peak_pair, peak_a, peak_b, peak_send2, peak_send3, f_pair, f_a, f_b,
    part_send, part_recv, loss_send, loss_pair, loss_send2, loss_y,
    load_sem, gather_sems, gather_send, scatter_sems, scatter_send, peak_sems, peak_send, misc_sems, misc_send,
):
    ctx, cls = lax.axis_index("ctx"), lax.axis_index("cls")
    x, z = lax.div(ctx, DEPTH), lax.rem(ctx, DEPTH)
    y, c = lax.div(cls, 2), lax.rem(cls, 2)
    a = y + c * (x - y)
    b = x + c * (y - x)

    def at(dx=0, dy=0, dz=0):
        return (
            lax.rem(x + dx, SIDE) * DEPTH + lax.rem(z + dz, DEPTH),
            lax.rem(y + dy, SIDE) * 2 + c,
        )

    def on_a(d):
        return at(dx=d * c, dy=d * (1 - c))

    def on_b(d, dz):
        return at(dx=d * (1 - c), dy=d * c, dz=dz)

    partner = (ctx, y * 2 + 1 - c)
    plane = [(d, dz) for d in range(SIDE) for dz in range(DEPTH) if d or dz]

    def send(src, dst, send_sem, recv_sem, to):
        pltpu.make_async_remote_copy(
            src_ref=src, dst_ref=dst, send_sem=send_sem, recv_sem=recv_sem,
            device_id=to, device_id_type=MESH,
        ).start()

    def take(sem, ref):
        pltpu.make_async_copy(ref, ref, sem).wait()

    load_tok = pltpu.make_async_copy(tokens_hbm, tok, load_sem.at[0])
    load_head = pltpu.make_async_copy(head_hbm, head, load_sem.at[1])
    load_tok.start()
    load_head.start()

    barrier = pltpu.get_barrier_semaphore()

    def greet(to):
        pl.semaphore_signal(barrier, inc=1, device_id=to, device_id_type=MESH)

    for d, dz in plane:
        greet(on_b(d, dz))
    for d in range(1, SIDE):
        greet(on_a(d))
    greet(partner)

    @pl.when(c == 1)
    def _():
        for d, dz in plane:
            if d and dz:
                greet(at(dx=d, dz=dz))

    pl.semaphore_wait(barrier, 35 + 21 * c)

    def split(rows):
        return jnp.concatenate([rows[:, :128], rows[:, 128:]], axis=0)

    def gather_begin(g, p, rows):
        g[c, a, b, z] = split(rows).astype(BF16)
        own = g.at[c, a, b, z]
        for d, dz in plane:
            send(own, own, gather_send.at[p, 0], gather_sems.at[p, d], on_b(d, dz))

    def gather_spread(g, p):
        for d in (0, 1, 3, 2):
            unit = g.at[c, a, lax.rem(b + SIDE - d, SIDE)]
            take(gather_sems.at[p, d], unit.at[pl.ds(0, 7)] if d == 0 else unit)
            for e in range(1, SIDE):
                span = d + c * (e - d)
                send(unit, unit, gather_send.at[p, 1], gather_sems.at[p, 4 + span], on_a(e))

    def gather_forward(g, p, j):
        at_x = lax.rem(x + SIDE - j, SIDE)

        @pl.when(c == 0)
        def _():
            take(gather_sems.at[p, 4 + j], g.at[0, 0, pl.ds(0, 3)])
            part = g.at[0, :, at_x]
            send(part, part, gather_send.at[p, 2], gather_sems.at[p, 8 + j], partner)

        @pl.when(c == 1)
        def _():
            if j:
                take(gather_sems.at[p, 4 + j], g.at[0, 0])
            part = g.at[1, at_x]
            send(part, part, gather_send.at[p, 2], gather_sems.at[p, 8 + j], partner)

    def project(g, p, j, first):
        at_x = lax.rem(x + SIDE - j, SIDE)
        take(gather_sems.at[p, 8 + j], g.at[0, 0])
        for zz in range(DEPTH):
            for yy in range(SIDE):
                even = g[0, yy, at_x, zz].astype(F32)
                odd = g[1, at_x, yy, zz].astype(F32)
                for half in range(2):
                    rows = slice(8 * half, 8 * half + 8)
                    col = 256 * zz + 128 * half
                    rhs[16 * yy : 16 * yy + 16, col : col + 128] = jnp.concatenate(
                        [even[rows], odd[rows]], axis=0
                    ).astype(BF16)
        cols = pl.ds(pl.multiple_of(at_x * SPAN, SPAN), SPAN)
        more = lax.dot_general(tok[:, cols], rhs[...], NT, preferred_element_type=F32)
        if first:
            scores[...] = more
        else:
            scores[...] += more

    def gather_project(g, p):
        gather_spread(g, p)
        ready = (0, 1, 3, 2)
        gather_forward(g, p, ready[0])
        for n in range(SIDE):
            if n + 1 < SIDE:
                gather_forward(g, p, ready[n + 1])
            project(g, p, ready[n], n == 0)

    def pair_begin(p, j, pair_send, pair_recv):
        cols = pl.ds(pl.multiple_of(lax.rem(x + j, SIDE) * SPAN, SPAN), SPAN)
        total[j] = jnp.dot(lhs[...], tok[:, cols], preferred_element_type=F32)
        for yy in range(SIDE):
            rows = pl.ds(pl.multiple_of(16 * yy + 8 * (1 - c), 8), 8)
            for zz in range(DEPTH):
                col = 256 * zz
                pair_send[j, yy, zz] = jnp.concatenate(
                    [total[j, rows, col : col + 128], total[j, rows, col + 128 : col + 256]], axis=0
                ).astype(BF16)
        send(pair_send.at[j], pair_recv.at[j], scatter_send.at[p, 0], scatter_sems.at[p, j], partner)

    def pair_end(p, j, pair_recv, a_send, a_recv, scaled):
        take(scatter_sems.at[p, j], pair_recv.at[j])
        for i in range(SIDE):
            yy = lax.rem(y + i, SIDE)
            rows = pl.ds(pl.multiple_of(16 * yy + 8 * c, 8), 8)
            for zz in range(DEPTH):
                col = 256 * zz
                came = pair_recv[j, yy, zz].astype(F32)
                lo, hi = total[j, rows, col : col + 128], total[j, rows, col + 128 : col + 256]
                if scaled:
                    mine, theirs = f_pair[0, rows], f_pair[1, rows]
                    lo, hi = lo * mine + came[:8] * theirs, hi * mine + came[8:] * theirs
                else:
                    lo, hi = lo + came[:8], hi + came[8:]
                a_send[j, i, zz] = jnp.concatenate([lo, hi], axis=0).astype(BF16)

        @pl.when(c == 0)
        def _():
            for i in range(1, SIDE):
                send(a_send.at[j, i], a_recv.at[i - 1, j], scatter_send.at[p, 1], scatter_sems.at[p, 4 + j], on_a(i))

        if j:

            @pl.when(c == 1)
            def _():
                send(a_send.at[j], a_recv.at[j - 1], scatter_send.at[p, 1], scatter_sems.at[p, 4 + j], on_a(j))

    def a_end(p, u, a_send, a_recv, b_send, b_recv, scaled):
        @pl.when(c == 0)
        def _():
            take(scatter_sems.at[p, 4 + u], a_recv.at[0, pl.ds(0, 3)])

        if u == ORDER[0]:

            @pl.when(c == 1)
            def _():
                for j in range(1, SIDE):
                    take(scatter_sems.at[p, 4 + j], a_recv.at[0])

        rows = pl.ds(pl.multiple_of(16 * lax.rem(y + c * u, SIDE) + 8 * c, 8), 8)
        for zz in range(DEPTH):
            parts = [a_send[u * (1 - c), u * c, zz]] + [a_recv[k, u, zz] for k in range(3)]
            lo = hi = None
            for k, part in enumerate(parts):
                part = part.astype(F32)
                low, high = part[:8], part[8:]
                if scaled:
                    factor = f_a[k, rows]
                    low, high = low * factor, high * factor
                lo, hi = (low, high) if lo is None else (lo + low, hi + high)
            b_send[u, zz] = jnp.concatenate([lo, hi], axis=0).astype(BF16)
        for dz in range(DEPTH):
            if u or dz:
                send(
                    b_send.at[u, lax.rem(z + dz, DEPTH)], b_recv.at[u * DEPTH + dz],
                    scatter_send.at[p, 2], scatter_sems.at[p, 8], on_b(u, dz),
                )

    def b_end(p, b_send, b_recv, scaled):
        take(scatter_sems.at[p, 8], b_recv.at[pl.ds(1, 31)])
        lo = hi = None
        for k in range(SIDE * DEPTH):
            part = (b_recv[k] if k else b_send[0, z]).astype(F32)
            low, high = part[:8], part[8:]
            if scaled:
                factor = f_b[k]
                low, high = low * factor, high * factor
            lo, hi = (low, high) if lo is None else (lo + low, hi + high)
        return jnp.concatenate([lo, hi], axis=1)

    def as_column(row):
        wide = jnp.concatenate([row] * 8, axis=0)
        lane = lax.broadcasted_iota(jnp.int32, (64, 128), 1)
        sub = lax.broadcasted_iota(jnp.int32, (64, 128), 0)
        column = jnp.sum(jnp.where(lane == sub, wide, 0.0), axis=1, keepdims=True)
        return jnp.broadcast_to(column, (64, 128))

    rhs[64:, :] = jnp.zeros((64, SPAN), BF16)
    gather_begin(gathered1, 0, query_ref[...].astype(F32))
    load_tok.wait()
    gather_project(gathered1, 0)

    count = tok.shape[0]
    place = (ctx * 8 + cls) * count + lax.broadcasted_iota(jnp.int32, (count, 128), 0)
    valid = place < doc_ref[0]
    masked = jnp.where(valid, scores[...], FAR)
    peak = jnp.max(masked, axis=0, keepdims=True)
    peak_own[...] = jnp.broadcast_to(peak, (8, 128))
    send(peak_own, peak_pair, peak_send.at[0], peak_sems.at[0], partner)
    soft = jnp.where(valid, jnp.exp(masked - peak), 0.0)
    weights[...] = soft
    lhs[...] = soft.T[:64].astype(BF16)

    first = (0, pair_send1, pair_recv1)
    pair_begin(0, ORDER[0], pair_send1, pair_recv1)
    take(peak_sems.at[0], peak_pair)
    peak2 = jnp.maximum(peak_own[...], peak_pair[...])
    peak_send2[...] = peak2
    for d in range(1, SIDE):
        send(peak_send2, peak_a.at[d - 1], peak_send.at[1], peak_sems.at[1], on_a(d))
    f_pair[0] = as_column(jnp.exp(peak_own[...] - peak2))
    f_pair[1] = as_column(jnp.exp(peak_pair[...] - peak2))
    for n in range(1, SIDE):
        pair_begin(0, ORDER[n], pair_send1, pair_recv1)
        pair_end(0, ORDER[n - 1], pair_recv1, a_send1, a_recv1, True)
    pair_end(0, ORDER[-1], pair_recv1, a_send1, a_recv1, True)
    take(peak_sems.at[1], peak_a)
    peak3 = peak_send2[...]
    for k in range(3):
        peak3 = jnp.maximum(peak3, peak_a[k])
    peak_send3[...] = peak3
    for d, dz in plane:
        send(peak_send3, peak_b.at[d * DEPTH + dz], peak_send.at[2], peak_sems.at[2], on_b(d, dz))
    f_a[0] = as_column(jnp.exp(peak_send2[...] - peak3))
    for k in range(3):
        f_a[k + 1] = as_column(jnp.exp(peak_a[k] - peak3))
    for u in ORDER:
        a_end(0, u, a_send1, a_recv1, b_send1, b_recv1, True)
    take(peak_sems.at[2], peak_b.at[pl.ds(1, 31)])
    peak_b[0] = peak_send3[...]
    top = jnp.max(peak_b[...], axis=0)
    lane8 = lax.broadcasted_iota(jnp.int32, (8, 128), 1)
    row8 = lax.broadcasted_iota(jnp.int32, (8, 128), 0)
    here = lane8 == row8 + (16 * y + 8 * c)
    for k in range(SIDE * DEPTH):
        factor = jnp.sum(jnp.where(here, jnp.exp(peak_b[k] - top), 0.0), axis=1, keepdims=True)
        f_b[k] = jnp.broadcast_to(factor, (8, 128))
    pooled = b_end(0, b_send1, b_recv1, True)

    load_head.wait()
    gain = gain_ref[...]
    lane512 = lax.broadcasted_iota(jnp.int32, (8, 512), 1)
    row512 = lax.broadcasted_iota(jnp.int32, (8, 512), 0)
    mine = (lane512 >= row512 * 64) & (lane512 < row512 * 64 + 64)
    low_half = lane8 < 64
    even_row = (row8 & 1) == 0
    active = (low_half & even_row) | (~low_half & ~even_row)

    def fold(wide):
        wide = jnp.where(mine, wide, 0.0)
        return wide[:, :128] + wide[:, 128:256] + wide[:, 256:384] + wide[:, 384:]

    product = jnp.dot((pooled * gain).astype(BF16), head[...], preferred_element_type=F32)
    square = jnp.sum(pooled * pooled, axis=1, keepdims=True)
    part_send[...] = jnp.where(active, fold(product), square)
    for d, dz in plane:
        send(part_send, part_recv.at[ctx], misc_send.at[0], misc_sems.at[0], at(dx=d, dz=dz))
    part_recv[ctx] = part_send[...]
    bias = fold(jnp.broadcast_to(bias_ref[...], (8, 512)))
    target = fold(jnp.broadcast_to(label_ref[...].astype(F32), (8, 512)))
    take(misc_sems.at[0], part_recv.at[pl.ds(0, 31)])
    raw = jnp.sum(part_recv[...], axis=0)
    squares = jnp.max(jnp.where(active, FAR, raw), axis=1, keepdims=True)
    inverse = lax.rsqrt(squares / (SPAN * SIDE) + 1e-05)
    logits = inverse * raw + bias
    grad = jnp.where(active, jax.nn.sigmoid(logits) - target, 0.0)
    inner = inverse * jnp.sum(jnp.where(active, grad * raw, 0.0), axis=1, keepdims=True) / (SPAN * SIDE)
    wide = jnp.where(mine, jnp.concatenate([grad] * 4, axis=1), 0.0)
    wide_hi = wide.astype(BF16).astype(F32)
    wide_lo = wide - wide_hi
    back = lax.dot_general(
        jnp.concatenate([wide_hi, wide_lo], axis=0).astype(BF16), head[...], NT, preferred_element_type=F32
    )
    normed_grad = (back[:8] + back[8:]) * gain
    unit = pooled * inverse
    pooled_grad = inverse * (normed_grad - unit * inner)

    gather_begin(gathered2, 1, pooled_grad)
    bias_grad_ref[...] = jnp.sum(wide, axis=0, keepdims=True)
    soft_plus = jnp.maximum(logits, 0.0) + jnp.log1p(jnp.exp(-jnp.abs(logits)))
    loss = jnp.where(active, soft_plus - target * logits, 0.0)
    loss = jnp.sum(jnp.sum(loss, axis=1, keepdims=True), axis=0, keepdims=True)
    loss_send[...] = jnp.broadcast_to(loss, (8, 128))
    send(loss_send, loss_pair, misc_send.at[1], misc_sems.at[1], partner)
    normed = unit * gain
    normed_hi = normed.astype(BF16).astype(F32)
    none = jnp.zeros((8, 256), F32)
    left = jnp.concatenate([normed_hi, normed - normed_hi, normed_hi, none], axis=0).astype(BF16)
    right = jnp.concatenate([wide_hi, wide_hi, wide_lo, jnp.zeros((8, 512), F32)], axis=0).astype(BF16)
    head_grad[...] = lax.dot_general(left, right, TN, preferred_element_type=F32)
    store_head = pltpu.make_async_copy(head_grad, head_grad_hbm, load_sem.at[2])
    store_head.start()
    take(misc_sems.at[1], loss_pair)
    loss_send2[...] = loss_send[...] + loss_pair[...]
    for d in range(1, SIDE):
        send(loss_send2, loss_y.at[y], misc_send.at[2], misc_sems.at[2], at(dy=d))
    loss_y[y] = loss_send2[...]
    own_share = jnp.exp(peak_own[...] - top)[:1]
    weights[...] = weights[...] * own_share
    gather_project(gathered2, 1)
    lhs[...] = (weights[...] * scores[...]).T[:64].astype(BF16)

    pair_begin(1, ORDER[0], pair_send2, pair_recv2)
    for n in range(1, SIDE):
        pair_begin(1, ORDER[n], pair_send2, pair_recv2)
        pair_end(1, ORDER[n - 1], pair_recv2, a_send2, a_recv2, False)
    pair_end(1, ORDER[-1], pair_recv2, a_send2, a_recv2, False)
    for u in ORDER:
        a_end(1, u, a_send2, a_recv2, b_send2, b_recv2, False)
    take(misc_sems.at[2], loss_y.at[pl.ds(0, 3)])
    loss_ref[...] = jnp.sum(loss_y[...], axis=0) / 4096.0

    for p, (g, pair_recv, a_recv, b_recv) in enumerate(
        ((gathered1, pair_recv1, a_recv1, b_recv1), (gathered2, pair_recv2, a_recv2, b_recv2))
    ):
        take(gather_send.at[p, 0], b_recv.at[pl.ds(0, 31)])
        take(gather_send.at[p, 1], g.at[0, pl.ds(0, 3)])
        take(gather_send.at[p, 2], g.at[0])
        take(scatter_send.at[p, 0], pair_recv)
        take(scatter_send.at[p, 1], a_recv)
        take(scatter_send.at[p, 2], b_recv.at[pl.ds(0, 31)])
    take(peak_send.at[0], peak_pair)
    take(peak_send.at[1], peak_a)
    take(peak_send.at[2], peak_b.at[pl.ds(0, 31)])
    take(misc_send.at[0], part_recv.at[pl.ds(0, 31)])
    take(misc_send.at[1], loss_pair)
    take(misc_send.at[2], loss_y.at[pl.ds(0, 3)])
    store_head.wait()
    query_grad_ref[...] = b_end(1, b_send2, b_recv2, False)


def shards(tokens, doc_length, queries, norm_gain, head_weight, head_bias, labels):
    count, width = tokens.shape
    rows, features = queries.shape
    attributes = head_bias.shape[0]
    vmem = pl.BlockSpec(memory_space=pltpu.VMEM)
    anywhere = pl.BlockSpec(memory_space=pl.ANY)
    tile, row = (16, 128), (8, 128)

    def exchange():
        return [
            pltpu.VMEM((SIDE, SIDE, DEPTH, *tile), BF16),
            pltpu.VMEM((SIDE, SIDE, DEPTH, *tile), BF16),
            pltpu.VMEM((SIDE, SIDE, DEPTH, *tile), BF16),
            pltpu.VMEM((SIDE - 1, SIDE, DEPTH, *tile), BF16),
            pltpu.VMEM((SIDE, DEPTH, *tile), BF16),
            pltpu.VMEM((SIDE * DEPTH, *tile), BF16),
        ]

    loss, query_grad, head_grad, bias_grad = pl.pallas_call(
        kernel,
        out_shape=(
            jax.ShapeDtypeStruct(row, F32),
            jax.ShapeDtypeStruct((rows, features), F32),
            jax.ShapeDtypeStruct(head_weight.shape, F32),
            jax.ShapeDtypeStruct((1, attributes), F32),
        ),
        in_specs=[
            pl.BlockSpec(memory_space=pltpu.SMEM),
            anywhere,
            vmem,
            vmem,
            anywhere,
            vmem,
            vmem,
        ],
        out_specs=(vmem, vmem, anywhere, vmem),
        scratch_shapes=[
            pltpu.VMEM((count, width), BF16),
            pltpu.VMEM(head_weight.shape, BF16),
            pltpu.VMEM(head_weight.shape, F32),
            pltpu.VMEM((2, SIDE, SIDE, DEPTH, *tile), BF16),
            pltpu.VMEM((2, SIDE, SIDE, DEPTH, *tile), BF16),
            pltpu.VMEM((128, SPAN), BF16),
            pltpu.VMEM((count, 128), F32),
            pltpu.VMEM((count, 128), F32),
            pltpu.VMEM((64, count), BF16),
            pltpu.VMEM((SIDE, 64, SPAN), F32),
            *exchange(),
            *exchange(),
            pltpu.VMEM(row, F32),
            pltpu.VMEM(row, F32),
            pltpu.VMEM((SIDE - 1, *row), F32),
            pltpu.VMEM((SIDE * DEPTH, *row), F32),
            pltpu.VMEM(row, F32),
            pltpu.VMEM(row, F32),
            pltpu.VMEM((2, 64, 128), F32),
            pltpu.VMEM((SIDE, 64, 128), F32),
            pltpu.VMEM((SIDE * DEPTH, *row), F32),
            pltpu.VMEM(row, F32),
            pltpu.VMEM((SIDE * DEPTH, *row), F32),
            pltpu.VMEM(row, F32),
            pltpu.VMEM(row, F32),
            pltpu.VMEM(row, F32),
            pltpu.VMEM((SIDE, *row), F32),
            pltpu.SemaphoreType.DMA((3,)),
            pltpu.SemaphoreType.DMA((2, 12)),
            pltpu.SemaphoreType.DMA((2, 3)),
            pltpu.SemaphoreType.DMA((2, 9)),
            pltpu.SemaphoreType.DMA((2, 3)),
            pltpu.SemaphoreType.DMA((3,)),
            pltpu.SemaphoreType.DMA((3,)),
            pltpu.SemaphoreType.DMA((3,)),
            pltpu.SemaphoreType.DMA((3,)),
        ],
        compiler_params=pltpu.CompilerParams(
            collective_id=0, has_side_effects=True, vmem_limit_bytes=52 * 2**20
        ),
        name="pooling_step",
    )(
        doc_length,
        tokens,
        queries,
        norm_gain.reshape(1, -1),
        head_weight,
        head_bias.reshape(1, -1),
        labels.reshape(1, -1),
    )
    return loss[0, 0], query_grad, head_grad, bias_grad.reshape(-1)


def solution(mesh):
    return jax.shard_map(
        shards,
        mesh=mesh,
        in_specs=(
            P(("ctx", "cls"), None),
            P(),
            P("cls", "ctx"),
            P("ctx"),
            P("ctx", "cls"),
            P("cls"),
            P("cls"),
        ),
        out_specs=(P(), P("cls", "ctx"), P("ctx", "cls"), P("cls")),
        check_vma=False,
    )
```

```python
import jax
import jax.numpy as jnp
from jax import lax
from jax.experimental import pallas as pl
from jax.experimental.pallas import tpu as pltpu
from jax.sharding import PartitionSpec as P

MESH = pl.DeviceIdType.MESH
F32, BF16 = jnp.float32, jnp.bfloat16
NT = (((1,), (1,)), ((), ()))
TN = (((0,), (0,)), ((), ()))
SIDE, DEPTH = 4, 8
SPAN = 2048
FAR = -1e30
ORDER = (2, 1, 3, 0)
READY = (0, 1, 3, 2)


def hops(d, dz):
    return min(d, SIDE - d) + min(dz, DEPTH - dz)


def kernel(
    doc_ref, tokens_hbm, query_hbm, gain_hbm, head_hbm, bias_hbm, label_hbm,
    loss_ref, query_grad_ref, normed_ref, wide_ref,
    tok, head, query_ref, gain_ref, bias_ref, label_ref, gathered1, gathered2, rhs, scores, weights, lhs, total,
    pair_send1, pair_recv1, a_send1, a_recv1, b_send1, b_recv1,
    pair_send2, pair_recv2, a_send2, a_recv2, b_send2, b_recv2,
    peak_own, peak_pair, peak_a, peak_b, peak_send2, peak_send3, f_pair, f_a, f_b,
    part_send, part_recv, loss_send, loss_pair, loss_send2, loss_y,
    load_sem, gather_sems, gather_send, scatter_sems, scatter_send, peak_sems, peak_send, misc_sems, misc_send,
):
    ctx, cls = lax.axis_index("ctx"), lax.axis_index("cls")
    x, z = ctx >> 3, ctx & 7
    y, c = cls >> 1, cls & 1
    a = y + c * (x - y)
    b = x + c * (y - x)

    x_at = [((x + d) & 3) * DEPTH for d in range(SIDE)]
    y_at = [((y + d) & 3) * 2 + c for d in range(SIDE)]
    z_at = [(z + d) & 7 for d in range(DEPTH)]
    x_if_b = [x_at[d] + c * (x_at[0] - x_at[d]) for d in range(SIDE)]
    y_if_b = [y_at[0] + c * (y_at[d] - y_at[0]) for d in range(SIDE)]
    x_if_a = [x_at[0] + c * (x_at[d] - x_at[0]) for d in range(SIDE)]
    y_if_a = [y_at[d] + c * (y_at[0] - y_at[d]) for d in range(SIDE)]

    def at(dx=0, dy=0, dz=0):
        return (x_at[dx] + z_at[dz], y_at[dy])

    def on_a(d):
        return (x_if_a[d] + z, y_if_a[d])

    def on_b(d, dz):
        return (x_if_b[d] + z_at[dz], y_if_b[d])

    partner = (ctx, y * 2 + 1 - c)
    plane = [(d, dz) for d in range(SIDE) for dz in range(DEPTH) if d or dz]
    plane.sort(key=lambda step: -hops(*step))

    def send(src, dst, send_sem, recv_sem, to):
        pltpu.make_async_remote_copy(
            src_ref=src, dst_ref=dst, send_sem=send_sem, recv_sem=recv_sem,
            device_id=to, device_id_type=MESH,
        ).start()

    def take(sem, ref):
        pltpu.make_async_copy(ref, ref, sem).wait()

    load_tok = pltpu.make_async_copy(tokens_hbm, tok, load_sem.at[0])
    load_query = pltpu.make_async_copy(query_hbm, query_ref, load_sem.at[1])
    load_rest = [
        pltpu.make_async_copy(src, dst, load_sem.at[2 + k])
        for k, (src, dst) in enumerate(
            ((head_hbm, head), (gain_hbm, gain_ref), (bias_hbm, bias_ref), (label_hbm, label_ref))
        )
    ]
    load_query.start()
    load_tok.start()
    for load in load_rest:
        load.start()

    barrier = pltpu.get_barrier_semaphore()

    def greet(to):
        pl.semaphore_signal(barrier, inc=1, device_id=to, device_id_type=MESH)

    for d, dz in plane:
        greet(on_b(d, dz))
    for d in range(1, SIDE):
        greet(on_a(d))
    greet(partner)

    pl.semaphore_wait(barrier, 35)

    def split(rows):
        return jnp.concatenate([rows[:, :128], rows[:, 128:]], axis=0)

    def gather_begin(g, p, rows):
        g[c, a, b, z] = split(rows).astype(BF16)
        own = g.at[c, a, b, z]
        for d, dz in sorted(plane, key=lambda step: (READY.index(step[0]), -hops(*step))):
            send(own, own, gather_send.at[p, 0], gather_sems.at[p, d], on_b(d, dz))

    def gather_spread(g, p):
        for d in READY:
            unit = g.at[c, a, (b + SIDE - d) & 3]
            take(gather_sems.at[p, d], unit.at[pl.ds(0, 7)] if d == 0 else unit)

            @pl.when(c == 0)
            def _():
                for e in (2, 1, 3):
                    send(unit, unit, gather_send.at[p, 2], gather_sems.at[p, 4 + d], on_a(e))

            @pl.when(c == 1)
            def _():
                for e in (1, 3, 2):
                    send(unit, unit, gather_send.at[p, 2], gather_sems.at[p, 4 + e], on_a(e))

    def gather_sent(g, p):
        take(gather_send.at[p, 0], b_recv1.at[pl.ds(0, 31)])
        take(gather_send.at[p, 1], g.at[0])
        take(gather_send.at[p, 2], g.at[0, pl.ds(0, 3)])

    def gather_forward(g, p, core, j):
        at_x = (x + SIDE - j) & 3

        @pl.when(c == core)
        def _():
            if core == 0:
                take(gather_sems.at[p, 4 + j], g.at[0, 0, pl.ds(0, 3)])
                part = g.at[0, :, at_x]
            else:
                if j:
                    take(gather_sems.at[p, 4 + j], g.at[0, 0])
                part = g.at[1, at_x]
            send(part, part, gather_send.at[p, 1], gather_sems.at[p, 8 + j], partner)

    def project(g, p, j, first):
        at_x = ((x + SIDE - j) & 3)
        take(gather_sems.at[p, 8 + j], g.at[0, 0])
        for zz in range(DEPTH):
            for yy in range(SIDE):
                even = g[0, yy, at_x, zz].astype(F32)
                odd = g[1, at_x, yy, zz].astype(F32)
                for half in range(2):
                    rows = slice(8 * half, 8 * half + 8)
                    col = 256 * zz + 128 * half
                    rhs[16 * yy : 16 * yy + 16, col : col + 128] = jnp.concatenate(
                        [even[rows], odd[rows]], axis=0
                    ).astype(BF16)
        cols = pl.ds(pl.multiple_of(at_x * SPAN, SPAN), SPAN)
        more = lax.dot_general(tok[:, cols], rhs[...], NT, preferred_element_type=F32)
        if first:
            scores[...] = more
        else:
            scores[...] += more

    def gather_project(g, p):
        gather_spread(g, p)
        gather_forward(g, p, 0, READY[0])
        gather_forward(g, p, 1, READY[0])
        for n, j in enumerate(READY):
            if n < 3:
                gather_forward(g, p, 0, READY[n + 1])
            if n in (1, 2):
                gather_forward(g, p, 1, READY[n + 1])
            project(g, p, j, n == 0)
            if n == 0:
                gather_forward(g, p, 1, READY[1])

    def pair_begin(p, j, pair_send, pair_recv):
        cols = pl.ds(pl.multiple_of(((x + j) & 3) * SPAN, SPAN), SPAN)
        total[j] = jnp.dot(lhs[...], tok[:, cols], preferred_element_type=F32)
        for yy in range(SIDE):
            rows = pl.ds(pl.multiple_of(16 * yy + 8 * (1 - c), 8), 8)
            for zz in range(DEPTH):
                col = 256 * zz
                pair_send[j, yy, zz] = jnp.concatenate(
                    [total[j, rows, col : col + 128], total[j, rows, col + 128 : col + 256]], axis=0
                ).astype(BF16)
        send(pair_send.at[j], pair_recv.at[j], scatter_send.at[p, 0], scatter_sems.at[p, j], partner)

    def pair_end(p, j, pair_recv, a_send, a_recv, scaled):
        take(scatter_sems.at[p, j], pair_recv.at[j])
        for i in range(SIDE):
            yy = ((y + i) & 3)
            rows = pl.ds(pl.multiple_of(16 * yy + 8 * c, 8), 8)
            for zz in range(DEPTH):
                col = 256 * zz
                came = pair_recv[j, yy, zz].astype(F32)
                lo, hi = total[j, rows, col : col + 128], total[j, rows, col + 128 : col + 256]
                if scaled:
                    mine, theirs = f_pair[0, rows], f_pair[1, rows]
                    lo, hi = lo * mine + came[:8] * theirs, hi * mine + came[8:] * theirs
                else:
                    lo, hi = lo + came[:8], hi + came[8:]
                a_send[j, i, zz] = jnp.concatenate([lo, hi], axis=0).astype(BF16)

        @pl.when(c == 0)
        def _():
            for i in range(1, SIDE):
                send(a_send.at[j, i], a_recv.at[i - 1, j], scatter_send.at[p, 1], scatter_sems.at[p, 4 + j], on_a(i))

        if j:

            @pl.when(c == 1)
            def _():
                send(a_send.at[j], a_recv.at[j - 1], scatter_send.at[p, 1], scatter_sems.at[p, 4 + j], on_a(j))

    def a_end(p, u, a_send, a_recv, b_send, b_recv, scaled):
        @pl.when(c == 0)
        def _():
            take(scatter_sems.at[p, 4 + u], a_recv.at[0, pl.ds(0, 3)])

        if u == ORDER[0]:

            @pl.when(c == 1)
            def _():
                for j in range(1, SIDE):
                    take(scatter_sems.at[p, 4 + j], a_recv.at[0])

        rows = pl.ds(pl.multiple_of(16 * ((y + c * u) & 3) + 8 * c, 8), 8)
        for zz in range(DEPTH):
            parts = [a_send[u * (1 - c), u * c, zz]] + [a_recv[k, u, zz] for k in range(3)]
            lo = hi = None
            for k, part in enumerate(parts):
                part = part.astype(F32)
                low, high = part[:8], part[8:]
                if scaled:
                    factor = f_a[k, rows]
                    low, high = low * factor, high * factor
                lo, hi = (low, high) if lo is None else (lo + low, hi + high)
            b_send[u, zz] = jnp.concatenate([lo, hi], axis=0).astype(BF16)
        for dz in sorted(range(DEPTH), key=lambda dz: -hops(u, dz)):
            if u or dz:
                send(
                    b_send.at[u, z_at[dz]], b_recv.at[u * DEPTH + dz],
                    scatter_send.at[p, 2], scatter_sems.at[p, 8], on_b(u, dz),
                )

    def b_end(p, b_send, b_recv, scaled):
        take(scatter_sems.at[p, 8], b_recv.at[pl.ds(1, 31)])
        lo = hi = None
        for k in range(SIDE * DEPTH):
            part = (b_recv[k] if k else b_send[0, z]).astype(F32)
            low, high = part[:8], part[8:]
            if scaled:
                factor = f_b[k]
                low, high = low * factor, high * factor
            lo, hi = (low, high) if lo is None else (lo + low, hi + high)
        return jnp.concatenate([lo, hi], axis=1)

    def as_column(row):
        wide = jnp.broadcast_to(row, (64, 128))
        lane = lax.broadcasted_iota(jnp.int32, (64, 128), 1)
        sub = lax.broadcasted_iota(jnp.int32, (64, 128), 0)
        column = jnp.sum(jnp.where(lane == sub, wide, 0.0), axis=1, keepdims=True)
        return jnp.broadcast_to(column, (64, 128))

    rhs[64:, :] = jnp.zeros((64, SPAN), BF16)
    load_query.wait()
    gather_begin(gathered1, 0, query_ref[...].astype(F32))
    load_tok.wait()
    gather_project(gathered1, 0)

    @pl.when(c == 1)
    def _():
        for d, dz in plane:
            if d and dz:
                greet(at(dx=d, dz=dz))

    count = tok.shape[0]
    place = (ctx * 8 + cls) * count + lax.broadcasted_iota(jnp.int32, (count, 128), 0)
    valid = place < doc_ref[0]
    masked = jnp.where(valid, scores[...], FAR)
    peak = jnp.max(masked, axis=0, keepdims=True)
    peak_own[...] = peak
    send(peak_own, peak_pair, peak_send.at[0], peak_sems.at[0], partner)
    soft = jnp.where(valid, jnp.exp(masked - peak), 0.0)
    weights[...] = soft
    lhs[...] = soft.T[:64].astype(BF16)

    first = (0, pair_send1, pair_recv1)
    pair_begin(0, ORDER[0], pair_send1, pair_recv1)
    take(peak_sems.at[0], peak_pair)
    peak2 = jnp.maximum(peak_own[...], peak_pair[...])
    peak_send2[...] = peak2
    for d in range(1, SIDE):
        send(peak_send2, peak_a.at[d - 1], peak_send.at[1], peak_sems.at[1], on_a(d))
    f_pair[0] = as_column(jnp.exp(peak_own[...] - peak2))
    f_pair[1] = as_column(jnp.exp(peak_pair[...] - peak2))
    for n in range(1, SIDE):
        pair_begin(0, ORDER[n], pair_send1, pair_recv1)
        pair_end(0, ORDER[n - 1], pair_recv1, a_send1, a_recv1, True)
    pair_end(0, ORDER[-1], pair_recv1, a_send1, a_recv1, True)
    take(peak_sems.at[1], peak_a)
    peak3 = peak_send2[...]
    for k in range(3):
        peak3 = jnp.maximum(peak3, peak_a[k])
    peak_send3[...] = peak3
    for d, dz in plane:
        send(peak_send3, peak_b.at[d * DEPTH + dz], peak_send.at[2], peak_sems.at[2], on_b(d, dz))
    f_a[0] = as_column(jnp.exp(peak_send2[...] - peak3))
    for k in range(3):
        f_a[k + 1] = as_column(jnp.exp(peak_a[k] - peak3))
    for u in ORDER:
        a_end(0, u, a_send1, a_recv1, b_send1, b_recv1, True)
    take(peak_sems.at[2], peak_b.at[pl.ds(1, 31)])
    peak_b[0] = peak_send3[...]
    top = peak_b[0]
    for k in range(1, SIDE * DEPTH):
        top = jnp.maximum(top, peak_b[k])
    lane8 = lax.broadcasted_iota(jnp.int32, (8, 128), 1)
    row8 = lax.broadcasted_iota(jnp.int32, (8, 128), 0)
    here = lane8 == row8 + (16 * y + 8 * c)
    for k in range(SIDE * DEPTH):
        factor = jnp.sum(jnp.where(here, jnp.broadcast_to(jnp.exp(peak_b[k] - top), (8, 128)), 0.0), axis=1, keepdims=True)
        f_b[k] = jnp.broadcast_to(factor, (8, 128))
    pooled = b_end(0, b_send1, b_recv1, True)

    for load in load_rest:
        load.wait()
    gain = gain_ref[...]
    lane512 = lax.broadcasted_iota(jnp.int32, (8, 512), 1)
    row512 = lax.broadcasted_iota(jnp.int32, (8, 512), 0)
    mine = (lane512 >= row512 * 64) & (lane512 < row512 * 64 + 64)
    diagonal = lane8 == row8

    def flat(wide):
        return jnp.sum(jnp.where(mine, wide, 0.0), axis=0, keepdims=True)

    product = flat(jnp.dot((pooled * gain).astype(BF16), head[...], preferred_element_type=F32))
    square = jnp.sum(pooled * pooled, axis=1, keepdims=True)
    square = jnp.sum(jnp.where(diagonal, square, 0.0), axis=0, keepdims=True)
    part_send[...] = jnp.concatenate([product[:, 128 * k : 128 * k + 128] for k in range(4)] + [square], axis=0)

    @pl.when(c == 1)
    def _():
        pl.semaphore_wait(barrier, 21)

    for d, dz in plane:
        send(part_send, part_recv.at[ctx], misc_send.at[0], misc_sems.at[0], at(dx=d, dz=dz))
    part_recv[ctx] = part_send[...]
    bias = bias_ref[...]
    target = label_ref[...].astype(F32)
    take(misc_sems.at[0], part_recv.at[pl.ds(0, 31)])
    whole = part_recv[0]
    for k in range(1, SIDE * DEPTH):
        whole = whole + part_recv[k]
    raw = jnp.concatenate([whole[k : k + 1] for k in range(4)], axis=1)
    squares = jnp.broadcast_to(whole[4:5], (8, 128))
    squares = jnp.sum(jnp.where(diagonal, squares, 0.0), axis=1, keepdims=True)
    inverse = lax.rsqrt(squares / (SPAN * SIDE) + 1e-05)
    logits = flat(jnp.broadcast_to(inverse, (8, 512))) * raw + bias
    grad = jax.nn.sigmoid(logits) - target
    wide = jnp.where(mine, jnp.broadcast_to(grad, (8, 512)), 0.0)
    inner = inverse * jnp.sum(wide * raw, axis=1, keepdims=True) / (SPAN * SIDE)
    wide_hi = wide.astype(BF16).astype(F32)
    wide_lo = wide - wide_hi
    back = lax.dot_general(
        jnp.concatenate([wide_hi, wide_lo], axis=0).astype(BF16), head[...], NT, preferred_element_type=F32
    )
    normed_grad = (back[:8] + back[8:]) * gain
    unit = pooled * inverse
    pooled_grad = inverse * (normed_grad - unit * inner)

    gather_begin(gathered2, 1, pooled_grad)
    normed_ref[...] = unit * gain
    wide_ref[...] = wide
    soft_plus = jnp.maximum(logits, 0.0) + jnp.log1p(jnp.exp(-jnp.abs(logits)))
    loss = jnp.sum(soft_plus - target * logits, axis=1, keepdims=True)
    loss_send[...] = jnp.broadcast_to(loss, (1, 128))
    send(loss_send, loss_pair, misc_send.at[1], misc_sems.at[1], partner)
    own_share = jnp.exp(peak_own[...] - top)
    weights[...] = weights[...] * own_share
    gather_project(gathered2, 1)
    take(misc_sems.at[1], loss_pair)
    loss_send2[...] = loss_send[...] + loss_pair[...]
    for d in range(1, SIDE):
        send(loss_send2, loss_y.at[y], misc_send.at[2], misc_sems.at[2], at(dy=d))
    loss_y[y] = loss_send2[...]
    lhs[...] = (weights[...] * scores[...]).T[:64].astype(BF16)

    pair_begin(1, ORDER[0], pair_send2, pair_recv2)
    for n in range(1, SIDE):
        pair_begin(1, ORDER[n], pair_send2, pair_recv2)
        pair_end(1, ORDER[n - 1], pair_recv2, a_send2, a_recv2, False)
    pair_end(1, ORDER[-1], pair_recv2, a_send2, a_recv2, False)
    for u in ORDER:
        a_end(1, u, a_send2, a_recv2, b_send2, b_recv2, False)
    take(misc_sems.at[2], loss_y.at[pl.ds(0, 3)])
    loss_ref[0, 0] = jnp.sum(loss_y[...], axis=0)[0, 0] / 4096.0

    for p, (g, pair_recv, a_recv, b_recv) in enumerate(
        ((gathered1, pair_recv1, a_recv1, b_recv1), (gathered2, pair_recv2, a_recv2, b_recv2))
    ):
        gather_sent(g, p)
        take(scatter_send.at[p, 0], pair_recv)
        take(scatter_send.at[p, 1], a_recv)
        take(scatter_send.at[p, 2], b_recv.at[pl.ds(0, 31)])
    take(peak_send.at[0], peak_pair)
    take(peak_send.at[1], peak_a)
    take(peak_send.at[2], peak_b.at[pl.ds(0, 31)])
    take(misc_send.at[0], part_recv.at[pl.ds(0, 31)])
    take(misc_send.at[1], loss_pair)
    take(misc_send.at[2], loss_y.at[pl.ds(0, 3)])
    query_grad_ref[...] = b_end(1, b_send2, b_recv2, False)


def deliver(
    wide_in, normed_in, query_in, loss_in, head_out, bias_out, query_out, loss_out,
    wide_ref, normed_ref, query_ref, loss_ref, head_ref, bias_ref, sems,
):
    pairs = ((wide_in, wide_ref), (normed_in, normed_ref), (query_in, query_ref), (loss_in, loss_ref))
    loads = [pltpu.make_async_copy(src, dst, sems.at[k]) for k, (src, dst) in enumerate(pairs)]
    pairs = ((head_ref, head_out), (bias_ref, bias_out), (query_ref, query_out), (loss_ref, loss_out))
    stores = [pltpu.make_async_copy(src, dst, sems.at[4 + k]) for k, (src, dst) in enumerate(pairs)]
    for load in loads:
        load.start()
    for k in (2, 3):
        loads[k].wait()
        stores[k].start()
    loads[0].wait()
    wide = wide_ref[...]
    bias_ref[...] = jnp.sum(wide, axis=0, keepdims=True)
    stores[1].start()
    loads[1].wait()
    normed = normed_ref[...]
    normed_hi, wide_hi = normed.astype(BF16).astype(F32), wide.astype(BF16).astype(F32)
    left = [normed_hi, normed - normed_hi, normed_hi, jnp.zeros_like(normed)]
    right = [wide_hi, wide_hi, wide - wide_hi, jnp.zeros_like(wide)]
    left, right = (jnp.concatenate(rows, axis=0).astype(BF16) for rows in (left, right))
    head_ref[...] = lax.dot_general(left, right, TN, preferred_element_type=F32)
    stores[0].start()
    for store in stores:
        store.wait()


def shards(tokens, doc_length, queries, norm_gain, head_weight, head_bias, labels):
    count, width = tokens.shape
    rows, features = queries.shape
    attributes = head_bias.shape[0]
    vmem = pl.BlockSpec(memory_space=pltpu.VMEM)
    hbm = pl.BlockSpec(memory_space=pltpu.HBM)
    tile, row = (16, 128), (8, 128)

    def exchange():
        return [
            pltpu.VMEM((SIDE, SIDE, DEPTH, *tile), BF16),
            pltpu.VMEM((SIDE, SIDE, DEPTH, *tile), BF16),
            pltpu.VMEM((SIDE, SIDE, DEPTH, *tile), BF16),
            pltpu.VMEM((SIDE - 1, SIDE, DEPTH, *tile), BF16),
            pltpu.VMEM((SIDE, DEPTH, *tile), BF16),
            pltpu.VMEM((SIDE * DEPTH, *tile), BF16),
        ]

    loss, query_grad, normed, wide = pl.pallas_call(
        kernel,
        out_shape=(
            jax.ShapeDtypeStruct((1, 1), F32),
            jax.ShapeDtypeStruct((rows, features), F32),
            jax.ShapeDtypeStruct((rows, features), F32),
            jax.ShapeDtypeStruct((rows, attributes), F32),
        ),
        in_specs=[
            pl.BlockSpec(memory_space=pltpu.SMEM),
            hbm,
            hbm,
            hbm,
            hbm,
            hbm,
            hbm,
        ],
        out_specs=(pl.BlockSpec(memory_space=pltpu.SMEM), vmem, vmem, vmem),
        scratch_shapes=[
            pltpu.VMEM((count, width), BF16),
            pltpu.VMEM(head_weight.shape, BF16),
            pltpu.VMEM(queries.shape, BF16),
            pltpu.VMEM((1, features), F32),
            pltpu.VMEM((1, attributes), F32),
            pltpu.VMEM((1, attributes), jnp.int32),
            pltpu.VMEM((2, SIDE, SIDE, DEPTH, *tile), BF16),
            pltpu.VMEM((2, SIDE, SIDE, DEPTH, *tile), BF16),
            pltpu.VMEM((128, SPAN), BF16),
            pltpu.VMEM((count, 128), F32),
            pltpu.VMEM((count, 128), F32),
            pltpu.VMEM((64, count), BF16),
            pltpu.VMEM((SIDE, 64, SPAN), F32),
            *exchange(),
            *exchange(),
            pltpu.VMEM((1, 128), F32),
            pltpu.VMEM((1, 128), F32),
            pltpu.VMEM((SIDE - 1, 1, 128), F32),
            pltpu.VMEM((SIDE * DEPTH, 1, 128), F32),
            pltpu.VMEM((1, 128), F32),
            pltpu.VMEM((1, 128), F32),
            pltpu.VMEM((2, 64, 128), F32),
            pltpu.VMEM((SIDE, 64, 128), F32),
            pltpu.VMEM((SIDE * DEPTH, *row), F32),
            pltpu.VMEM((5, 128), F32),
            pltpu.VMEM((SIDE * DEPTH, 5, 128), F32),
            pltpu.VMEM((1, 128), F32),
            pltpu.VMEM((1, 128), F32),
            pltpu.VMEM((1, 128), F32),
            pltpu.VMEM((SIDE, 1, 128), F32),
            pltpu.SemaphoreType.DMA((6,)),
            pltpu.SemaphoreType.DMA((2, 12)),
            pltpu.SemaphoreType.DMA((2, 3)),
            pltpu.SemaphoreType.DMA((2, 9)),
            pltpu.SemaphoreType.DMA((2, 3)),
            pltpu.SemaphoreType.DMA((3,)),
            pltpu.SemaphoreType.DMA((3,)),
            pltpu.SemaphoreType.DMA((3,)),
            pltpu.SemaphoreType.DMA((3,)),
        ],
        compiler_params=pltpu.CompilerParams(
            collective_id=0, has_side_effects=True, vmem_limit_bytes=63 * 2**20
        ),
        name="pooling_step",
    )(
        doc_length,
        tokens,
        queries,
        norm_gain.reshape(1, -1),
        head_weight,
        head_bias.reshape(1, -1),
        labels.reshape(1, -1),
    )
    sizes = ((rows, attributes), (rows, features), (rows, features), (1, 1), head_weight.shape, (1, attributes))
    outputs = (sizes[4], sizes[5], sizes[2], sizes[3])
    head_grad, bias_grad, query_grad, loss = pl.pallas_call(
        deliver,
        out_shape=tuple(jax.ShapeDtypeStruct(size, F32) for size in outputs),
        in_specs=[hbm] * 4,
        out_specs=(hbm,) * 4,
        scratch_shapes=[pltpu.VMEM(size, F32) for size in sizes] + [pltpu.SemaphoreType.DMA((8,))],
        compiler_params=pltpu.CompilerParams(vmem_limit_bytes=63 * 2**20),
        name="deliver",
    )(wide, normed, query_grad, loss)
    return loss[0, 0], query_grad, head_grad, bias_grad.reshape(-1)


def solution(mesh):
    return jax.shard_map(
        shards,
        mesh=mesh,
        in_specs=(
            P(("ctx", "cls"), None),
            P(),
            P("cls", "ctx"),
            P("ctx"),
            P("ctx", "cls"),
            P("cls"),
            P("cls"),
        ),
        out_specs=(P(), P("cls", "ctx"), P("ctx", "cls"), P("cls")),
        check_vma=False,
    )
```

```python
import jax
import jax.numpy as jnp
from jax import lax
from jax.experimental import pallas as pl
from jax.experimental.pallas import tpu as pltpu
from jax.sharding import PartitionSpec as P

MESH = pl.DeviceIdType.MESH
F32, BF16 = jnp.float32, jnp.bfloat16
NT = (((1,), (1,)), ((), ()))
TN = (((0,), (0,)), ((), ()))
SIDE, DEPTH = 4, 8
SPAN = 2048
FAR = -1e30
ORDER = (2, 1, 3, 0)
READY = (0, 1, 3, 2)


def hops(d, dz):
    return min(d, SIDE - d) + min(dz, DEPTH - dz)


def kernel(
    doc_hbm, tokens_hbm, query_hbm, gain_hbm, head_hbm, bias_hbm, label_hbm,
    loss_ref, query_grad_ref, normed_ref, wide_ref,
    tok, head, doc_ref, query_ref, gain_ref, bias_ref, label_ref, gathered1, gathered2, rhs, scores, weights, lhs, total,
    pair_send1, pair_recv1, a_send1, a_recv1, b_send1, b_recv1,
    pair_send2, pair_recv2, a_send2, a_recv2, b_send2, b_recv2,
    peak_own, peak_pair, peak_a, peak_b, peak_send2, peak_send3, f_pair, f_a, f_b,
    part_send, part_recv, loss_send, loss_pair, loss_send2, loss_y,
    load_sem, gather_sems, gather_send, scatter_sems, scatter_send, peak_sems, peak_send, misc_sems, misc_send,
):
    ctx, cls = lax.axis_index("ctx"), lax.axis_index("cls")
    x, z = ctx >> 3, ctx & 7
    y, c = cls >> 1, cls & 1
    a = y + c * (x - y)
    b = x + c * (y - x)

    x_at = [((x + d) & 3) * DEPTH for d in range(SIDE)]
    y_at = [((y + d) & 3) * 2 + c for d in range(SIDE)]
    z_at = [(z + d) & 7 for d in range(DEPTH)]
    x_if_b = [x_at[d] + c * (x_at[0] - x_at[d]) for d in range(SIDE)]
    y_if_b = [y_at[0] + c * (y_at[d] - y_at[0]) for d in range(SIDE)]
    x_if_a = [x_at[0] + c * (x_at[d] - x_at[0]) for d in range(SIDE)]
    y_if_a = [y_at[d] + c * (y_at[0] - y_at[d]) for d in range(SIDE)]

    def at(dx=0, dy=0, dz=0):
        return (x_at[dx] + z_at[dz], y_at[dy])

    def on_a(d):
        return (x_if_a[d] + z, y_if_a[d])

    def on_b(d, dz):
        return (x_if_b[d] + z_at[dz], y_if_b[d])

    partner = (ctx, y * 2 + 1 - c)
    plane = [(d, dz) for d in range(SIDE) for dz in range(DEPTH) if d or dz]
    plane.sort(key=lambda step: -hops(*step))

    def send(src, dst, send_sem, recv_sem, to):
        pltpu.make_async_remote_copy(
            src_ref=src, dst_ref=dst, send_sem=send_sem, recv_sem=recv_sem,
            device_id=to, device_id_type=MESH,
        ).start()

    def take(sem, ref):
        pltpu.make_async_copy(ref, ref, sem).wait()

    load_tok = pltpu.make_async_copy(tokens_hbm, tok, load_sem.at[0])
    load_query = pltpu.make_async_copy(query_hbm, query_ref, load_sem.at[1])
    load_rest = [
        pltpu.make_async_copy(src, dst, load_sem.at[2 + k])
        for k, (src, dst) in enumerate(
            ((head_hbm, head), (gain_hbm, gain_ref), (bias_hbm, bias_ref), (label_hbm, label_ref), (doc_hbm, doc_ref))
        )
    ]
    load_query.start()
    load_tok.start()
    for load in load_rest:
        load.start()

    barrier = pltpu.get_barrier_semaphore()

    def greet(to):
        pl.semaphore_signal(barrier, inc=1, device_id=to, device_id_type=MESH)

    for d, dz in plane:
        greet(at(dx=d, dz=dz))
    for d in range(1, SIDE):
        greet(at(dy=d))
    greet(partner)

    pl.semaphore_wait(barrier, 35)

    def split(rows):
        return jnp.concatenate([rows[:, :128], rows[:, 128:]], axis=0)

    def gather_begin(g, p, rows):
        g[c, y, x, z] = split(rows).astype(BF16)
        own = g.at[c, y, x, z]
        for d, dz in sorted(plane, key=lambda step: (READY.index(step[0]), -hops(*step))):
            send(own, own, gather_send.at[p, 0], gather_sems.at[p, d], at(dx=d, dz=dz))

    def gather_spread(g, p):
        for d in READY:
            unit = g.at[c, y, (x + SIDE - d) & 3]
            take(gather_sems.at[p, d], unit.at[pl.ds(0, 7)] if d == 0 else unit)
            for e in (2, 1, 3):
                send(unit, unit, gather_send.at[p, 2], gather_sems.at[p, 4 + d], at(dy=e))

    def gather_sent(g, p):
        take(gather_send.at[p, 0], b_recv1.at[pl.ds(0, 31)])
        take(gather_send.at[p, 1], g.at[0])
        take(gather_send.at[p, 2], g.at[0, pl.ds(0, 3)])

    def gather_forward(g, p, j):
        take(gather_sems.at[p, 4 + j], g.at[0, 0, pl.ds(0, 3)])
        part = g.at[c, :, (x + SIDE - j) & 3]
        send(part, part, gather_send.at[p, 1], gather_sems.at[p, 8 + j], partner)

    def project(g, p, j, first):
        at_x = ((x + SIDE - j) & 3)
        take(gather_sems.at[p, 8 + j], g.at[0, 0])
        for zz in range(DEPTH):
            for yy in range(SIDE):
                even = g[0, yy, at_x, zz].astype(F32)
                odd = g[1, yy, at_x, zz].astype(F32)
                for half in range(2):
                    rows = slice(8 * half, 8 * half + 8)
                    col = 256 * zz + 128 * half
                    rhs[16 * yy : 16 * yy + 16, col : col + 128] = jnp.concatenate(
                        [even[rows], odd[rows]], axis=0
                    ).astype(BF16)
        cols = pl.ds(pl.multiple_of(at_x * SPAN, SPAN), SPAN)
        more = lax.dot_general(tok[:, cols], rhs[...], NT, preferred_element_type=F32)
        if first:
            scores[...] = more
        else:
            scores[...] += more

    def gather_project(g, p):
        gather_spread(g, p)
        gather_forward(g, p, READY[0])
        for n, j in enumerate(READY):
            if n < 3:
                gather_forward(g, p, READY[n + 1])
            project(g, p, j, n == 0)

    def pair_begin(p, j, pair_send, pair_recv):
        cols = pl.ds(pl.multiple_of(((x + j) & 3) * SPAN, SPAN), SPAN)
        total[j] = jnp.dot(lhs[...], tok[:, cols], preferred_element_type=F32)
        for yy in range(SIDE):
            rows = pl.ds(pl.multiple_of(16 * yy + 8 * (1 - c), 8), 8)
            for zz in range(DEPTH):
                col = 256 * zz
                pair_send[j, yy, zz] = jnp.concatenate(
                    [total[j, rows, col : col + 128], total[j, rows, col + 128 : col + 256]], axis=0
                ).astype(BF16)
        send(pair_send.at[j], pair_recv.at[j], scatter_send.at[p, 0], scatter_sems.at[p, j], partner)

    def pair_end(p, j, pair_recv, a_send, a_recv, scaled):
        take(scatter_sems.at[p, j], pair_recv.at[j])
        for i in range(SIDE):
            yy = ((y + i) & 3)
            rows = pl.ds(pl.multiple_of(16 * yy + 8 * c, 8), 8)
            for zz in range(DEPTH):
                col = 256 * zz
                came = pair_recv[j, yy, zz].astype(F32)
                lo, hi = total[j, rows, col : col + 128], total[j, rows, col + 128 : col + 256]
                if scaled:
                    mine, theirs = f_pair[0, rows], f_pair[1, rows]
                    lo, hi = lo * mine + came[:8] * theirs, hi * mine + came[8:] * theirs
                else:
                    lo, hi = lo + came[:8], hi + came[8:]
                a_send[j, i, zz] = jnp.concatenate([lo, hi], axis=0).astype(BF16)

        @pl.when(c == 0)
        def _():
            for i in range(1, SIDE):
                send(a_send.at[j, i], a_recv.at[i - 1, j], scatter_send.at[p, 1], scatter_sems.at[p, 4 + j], on_a(i))

        if j:

            @pl.when(c == 1)
            def _():
                send(a_send.at[j], a_recv.at[j - 1], scatter_send.at[p, 1], scatter_sems.at[p, 4 + j], on_a(j))

    def a_end(p, u, a_send, a_recv, b_send, b_recv, scaled):
        @pl.when(c == 0)
        def _():
            take(scatter_sems.at[p, 4 + u], a_recv.at[0, pl.ds(0, 3)])

        if u == ORDER[0]:

            @pl.when(c == 1)
            def _():
                for j in range(1, SIDE):
                    take(scatter_sems.at[p, 4 + j], a_recv.at[0])

        rows = pl.ds(pl.multiple_of(16 * ((y + c * u) & 3) + 8 * c, 8), 8)
        for zz in range(DEPTH):
            parts = [a_send[u * (1 - c), u * c, zz]] + [a_recv[k, u, zz] for k in range(3)]
            lo = hi = None
            for k, part in enumerate(parts):
                part = part.astype(F32)
                low, high = part[:8], part[8:]
                if scaled:
                    factor = f_a[k, rows]
                    low, high = low * factor, high * factor
                lo, hi = (low, high) if lo is None else (lo + low, hi + high)
            b_send[u, zz] = jnp.concatenate([lo, hi], axis=0).astype(BF16)
        for dz in sorted(range(DEPTH), key=lambda dz: -hops(u, dz)):
            if u or dz:
                send(
                    b_send.at[u, z_at[dz]], b_recv.at[u * DEPTH + dz],
                    scatter_send.at[p, 2], scatter_sems.at[p, 8], on_b(u, dz),
                )

    def b_end(p, b_send, b_recv, scaled):
        take(scatter_sems.at[p, 8], b_recv.at[pl.ds(1, 31)])
        lo = hi = None
        for k in range(SIDE * DEPTH):
            part = (b_recv[k] if k else b_send[0, z]).astype(F32)
            low, high = part[:8], part[8:]
            if scaled:
                factor = f_b[k]
                low, high = low * factor, high * factor
            lo, hi = (low, high) if lo is None else (lo + low, hi + high)
        return jnp.concatenate([lo, hi], axis=1)

    def as_column(row):
        wide = jnp.broadcast_to(row, (64, 128))
        lane = lax.broadcasted_iota(jnp.int32, (64, 128), 1)
        sub = lax.broadcasted_iota(jnp.int32, (64, 128), 0)
        column = jnp.sum(jnp.where(lane == sub, wide, 0.0), axis=1, keepdims=True)
        return jnp.broadcast_to(column, (64, 128))

    rhs[64:, :] = jnp.zeros((64, SPAN), BF16)
    load_query.wait()
    gather_begin(gathered1, 0, query_ref[...].astype(F32))
    for load in [load_tok] + load_rest:
        load.wait()
    gather_project(gathered1, 0)

    @pl.when(c == 1)
    def _():
        for d, dz in plane:
            if d and dz:
                greet(at(dy=d, dz=dz))

    count = tok.shape[0]
    place = (ctx * 8 + cls) * count + lax.broadcasted_iota(jnp.int32, (count, 128), 0)
    valid = place < doc_ref[...]
    masked = jnp.where(valid, scores[...], FAR)
    peak = jnp.max(masked, axis=0, keepdims=True)
    peak_own[...] = peak
    send(peak_own, peak_pair, peak_send.at[0], peak_sems.at[0], partner)
    soft = jnp.where(valid, jnp.exp(masked - peak), 0.0)
    weights[...] = soft
    lhs[...] = soft.astype(BF16).T[:64]

    first = (0, pair_send1, pair_recv1)
    pair_begin(0, ORDER[0], pair_send1, pair_recv1)
    take(peak_sems.at[0], peak_pair)
    peak2 = jnp.maximum(peak_own[...], peak_pair[...])
    peak_send2[...] = peak2
    for d in range(1, SIDE):
        send(peak_send2, peak_a.at[d - 1], peak_send.at[1], peak_sems.at[1], on_a(d))
    f_pair[0] = as_column(jnp.exp(peak_own[...] - peak2))
    f_pair[1] = as_column(jnp.exp(peak_pair[...] - peak2))
    for n in range(1, SIDE):
        pair_begin(0, ORDER[n], pair_send1, pair_recv1)
        pair_end(0, ORDER[n - 1], pair_recv1, a_send1, a_recv1, True)
    pair_end(0, ORDER[-1], pair_recv1, a_send1, a_recv1, True)
    take(peak_sems.at[1], peak_a)
    peak3 = peak_send2[...]
    for k in range(3):
        peak3 = jnp.maximum(peak3, peak_a[k])
    peak_send3[...] = peak3
    @pl.when(c == 1)
    def _():
        pl.semaphore_wait(barrier, 21)

    for d, dz in plane:
        send(peak_send3, peak_b.at[d * DEPTH + dz], peak_send.at[2], peak_sems.at[2], on_b(d, dz))
    f_a[0] = as_column(jnp.exp(peak_send2[...] - peak3))
    for k in range(3):
        f_a[k + 1] = as_column(jnp.exp(peak_a[k] - peak3))
    for u in ORDER:
        a_end(0, u, a_send1, a_recv1, b_send1, b_recv1, True)
    take(peak_sems.at[2], peak_b.at[pl.ds(1, 31)])
    peak_b[0] = peak_send3[...]
    top = peak_b[0]
    for k in range(1, SIDE * DEPTH):
        top = jnp.maximum(top, peak_b[k])
    lane8 = lax.broadcasted_iota(jnp.int32, (8, 128), 1)
    row8 = lax.broadcasted_iota(jnp.int32, (8, 128), 0)
    here = lane8 == row8 + (16 * y + 8 * c)
    for k in range(SIDE * DEPTH):
        factor = jnp.sum(jnp.where(here, jnp.broadcast_to(jnp.exp(peak_b[k] - top), (8, 128)), 0.0), axis=1, keepdims=True)
        f_b[k] = jnp.broadcast_to(factor, (8, 128))
    pooled = b_end(0, b_send1, b_recv1, True)

    gain = gain_ref[...]
    lane512 = lax.broadcasted_iota(jnp.int32, (8, 512), 1)
    row512 = lax.broadcasted_iota(jnp.int32, (8, 512), 0)
    mine = (lane512 >= row512 * 64) & (lane512 < row512 * 64 + 64)
    diagonal = lane8 == row8

    def flat(wide):
        return jnp.sum(jnp.where(mine, wide, 0.0), axis=0, keepdims=True)

    product = flat(jnp.dot((pooled * gain).astype(BF16), head[...], preferred_element_type=F32))
    square = jnp.sum(pooled * pooled, axis=1, keepdims=True)
    square = jnp.sum(jnp.where(diagonal, square, 0.0), axis=0, keepdims=True)
    part_send[...] = jnp.concatenate([product[:, 128 * k : 128 * k + 128] for k in range(4)] + [square], axis=0)
    for d, dz in plane:
        send(part_send, part_recv.at[ctx], misc_send.at[0], misc_sems.at[0], at(dx=d, dz=dz))
    part_recv[ctx] = part_send[...]
    bias = bias_ref[...]
    target = label_ref[...].astype(F32)
    take(misc_sems.at[0], part_recv.at[pl.ds(0, 31)])
    whole = part_recv[0]
    for k in range(1, SIDE * DEPTH):
        whole = whole + part_recv[k]
    raw = jnp.concatenate([whole[k : k + 1] for k in range(4)], axis=1)
    squares = jnp.broadcast_to(whole[4:5], (8, 128))
    squares = jnp.sum(jnp.where(diagonal, squares, 0.0), axis=1, keepdims=True)
    inverse = lax.rsqrt(squares / (SPAN * SIDE) + 1e-05)
    logits = flat(jnp.broadcast_to(inverse, (8, 512))) * raw + bias
    grad = jax.nn.sigmoid(logits) - target
    wide = jnp.where(mine, jnp.broadcast_to(grad, (8, 512)), 0.0)
    inner = inverse * jnp.sum(wide * raw, axis=1, keepdims=True) / (SPAN * SIDE)
    wide_hi = wide.astype(BF16).astype(F32)
    wide_lo = wide - wide_hi
    back = lax.dot_general(
        jnp.concatenate([wide_hi, wide_lo], axis=0).astype(BF16), head[...], NT, preferred_element_type=F32
    )
    normed_grad = (back[:8] + back[8:]) * gain
    unit = pooled * inverse
    pooled_grad = inverse * (normed_grad - unit * inner)

    gather_begin(gathered2, 1, pooled_grad)
    normed_ref[...] = unit * gain
    wide_ref[...] = wide
    soft_plus = jnp.maximum(logits, 0.0) + jnp.log1p(jnp.exp(-jnp.abs(logits)))
    loss = jnp.sum(soft_plus - target * logits, axis=1, keepdims=True)
    loss_send[...] = jnp.broadcast_to(loss, (1, 128))
    send(loss_send, loss_pair, misc_send.at[1], misc_sems.at[1], partner)
    own_share = jnp.exp(peak_own[...] - top)
    weights[...] = weights[...] * own_share
    gather_project(gathered2, 1)
    take(misc_sems.at[1], loss_pair)
    loss_send2[...] = loss_send[...] + loss_pair[...]
    for d in range(1, SIDE):
        send(loss_send2, loss_y.at[y], misc_send.at[2], misc_sems.at[2], at(dy=d))
    loss_y[y] = loss_send2[...]
    lhs[...] = (weights[...] * scores[...]).astype(BF16).T[:64]

    pair_begin(1, ORDER[0], pair_send2, pair_recv2)
    for n in range(1, SIDE):
        pair_begin(1, ORDER[n], pair_send2, pair_recv2)
        pair_end(1, ORDER[n - 1], pair_recv2, a_send2, a_recv2, False)
    pair_end(1, ORDER[-1], pair_recv2, a_send2, a_recv2, False)
    for u in ORDER:
        a_end(1, u, a_send2, a_recv2, b_send2, b_recv2, False)
    take(misc_sems.at[2], loss_y.at[pl.ds(0, 3)])
    loss_ref[0, 0] = jnp.sum(loss_y[...], axis=0)[0, 0] / 4096.0

    for p, (g, pair_recv, a_recv, b_recv) in enumerate(
        ((gathered1, pair_recv1, a_recv1, b_recv1), (gathered2, pair_recv2, a_recv2, b_recv2))
    ):
        gather_sent(g, p)
        take(scatter_send.at[p, 0], pair_recv)
        take(scatter_send.at[p, 1], a_recv)
        take(scatter_send.at[p, 2], b_recv.at[pl.ds(0, 31)])
    take(peak_send.at[0], peak_pair)
    take(peak_send.at[1], peak_a)
    take(peak_send.at[2], peak_b.at[pl.ds(0, 31)])
    take(misc_send.at[0], part_recv.at[pl.ds(0, 31)])
    take(misc_send.at[1], loss_pair)
    take(misc_send.at[2], loss_y.at[pl.ds(0, 3)])
    query_grad_ref[...] = b_end(1, b_send2, b_recv2, False)


def deliver(
    wide_in, normed_in, query_in, loss_in, head_out, bias_out, query_out, loss_out,
    wide_ref, normed_ref, query_ref, loss_ref, head_ref, bias_ref, sems,
):
    pairs = ((wide_in, wide_ref), (normed_in, normed_ref), (query_in, query_ref), (loss_in, loss_ref))
    loads = [pltpu.make_async_copy(src, dst, sems.at[k]) for k, (src, dst) in enumerate(pairs)]
    pairs = ((head_ref, head_out), (bias_ref, bias_out), (query_ref, query_out), (loss_ref, loss_out))
    stores = [pltpu.make_async_copy(src, dst, sems.at[4 + k]) for k, (src, dst) in enumerate(pairs)]
    for load in loads:
        load.start()
    for k in (2, 3):
        loads[k].wait()
        stores[k].start()
    loads[0].wait()
    wide = wide_ref[...]
    bias_ref[...] = jnp.sum(wide, axis=0, keepdims=True)
    stores[1].start()
    loads[1].wait()
    normed = normed_ref[...]
    normed_hi, wide_hi = normed.astype(BF16).astype(F32), wide.astype(BF16).astype(F32)
    left = [normed_hi, normed - normed_hi, normed_hi, jnp.zeros_like(normed)]
    right = [wide_hi, wide_hi, wide - wide_hi, jnp.zeros_like(wide)]
    left, right = (jnp.concatenate(rows, axis=0).astype(BF16) for rows in (left, right))
    head_ref[...] = lax.dot_general(left, right, TN, preferred_element_type=F32)
    stores[0].start()
    for store in stores:
        store.wait()


def shards(tokens, doc_length, queries, norm_gain, head_weight, head_bias, labels):
    count, width = tokens.shape
    rows, features = queries.shape
    attributes = head_bias.shape[0]
    vmem = pl.BlockSpec(memory_space=pltpu.VMEM)
    hbm = pl.BlockSpec(memory_space=pltpu.HBM)
    tile, row = (16, 128), (8, 128)

    def exchange():
        return [
            pltpu.VMEM((SIDE, SIDE, DEPTH, *tile), BF16),
            pltpu.VMEM((SIDE, SIDE, DEPTH, *tile), BF16),
            pltpu.VMEM((SIDE, SIDE, DEPTH, *tile), BF16),
            pltpu.VMEM((SIDE - 1, SIDE, DEPTH, *tile), BF16),
            pltpu.VMEM((SIDE, DEPTH, *tile), BF16),
            pltpu.VMEM((SIDE * DEPTH, *tile), BF16),
        ]

    loss, query_grad, normed, wide = pl.pallas_call(
        kernel,
        out_shape=(
            jax.ShapeDtypeStruct((1, 1), F32),
            jax.ShapeDtypeStruct((rows, features), F32),
            jax.ShapeDtypeStruct((rows, features), F32),
            jax.ShapeDtypeStruct((rows, attributes), F32),
        ),
        in_specs=[
            hbm,
            hbm,
            hbm,
            hbm,
            hbm,
            hbm,
            hbm,
        ],
        out_specs=(pl.BlockSpec(memory_space=pltpu.SMEM), vmem, vmem, vmem),
        scratch_shapes=[
            pltpu.VMEM((count, width), BF16),
            pltpu.VMEM(head_weight.shape, BF16),
            pltpu.VMEM((1, 1), jnp.int32),
            pltpu.VMEM(queries.shape, BF16),
            pltpu.VMEM((1, features), F32),
            pltpu.VMEM((1, attributes), F32),
            pltpu.VMEM((1, attributes), jnp.int32),
            pltpu.VMEM((2, SIDE, SIDE, DEPTH, *tile), BF16),
            pltpu.VMEM((2, SIDE, SIDE, DEPTH, *tile), BF16),
            pltpu.VMEM((128, SPAN), BF16),
            pltpu.VMEM((count, 128), F32),
            pltpu.VMEM((count, 128), F32),
            pltpu.VMEM((64, count), BF16),
            pltpu.VMEM((SIDE, 64, SPAN), F32),
            *exchange(),
            *exchange(),
            pltpu.VMEM((1, 128), F32),
            pltpu.VMEM((1, 128), F32),
            pltpu.VMEM((SIDE - 1, 1, 128), F32),
            pltpu.VMEM((SIDE * DEPTH, 1, 128), F32),
            pltpu.VMEM((1, 128), F32),
            pltpu.VMEM((1, 128), F32),
            pltpu.VMEM((2, 64, 128), F32),
            pltpu.VMEM((SIDE, 64, 128), F32),
            pltpu.VMEM((SIDE * DEPTH, *row), F32),
            pltpu.VMEM((5, 128), F32),
            pltpu.VMEM((SIDE * DEPTH, 5, 128), F32),
            pltpu.VMEM((1, 128), F32),
            pltpu.VMEM((1, 128), F32),
            pltpu.VMEM((1, 128), F32),
            pltpu.VMEM((SIDE, 1, 128), F32),
            pltpu.SemaphoreType.DMA((7,)),
            pltpu.SemaphoreType.DMA((2, 12)),
            pltpu.SemaphoreType.DMA((2, 3)),
            pltpu.SemaphoreType.DMA((2, 9)),
            pltpu.SemaphoreType.DMA((2, 3)),
            pltpu.SemaphoreType.DMA((3,)),
            pltpu.SemaphoreType.DMA((3,)),
            pltpu.SemaphoreType.DMA((3,)),
            pltpu.SemaphoreType.DMA((3,)),
        ],
        compiler_params=pltpu.CompilerParams(
            collective_id=0, has_side_effects=True, vmem_limit_bytes=63 * 2**20
        ),
        name="pooling_step",
    )(
        doc_length.reshape(1, 1),
        tokens,
        queries,
        norm_gain.reshape(1, -1),
        head_weight,
        head_bias.reshape(1, -1),
        labels.reshape(1, -1),
    )
    sizes = ((rows, attributes), (rows, features), (rows, features), (1, 1), head_weight.shape, (1, attributes))
    outputs = (sizes[4], sizes[5], sizes[2], sizes[3])
    head_grad, bias_grad, query_grad, loss = pl.pallas_call(
        deliver,
        out_shape=tuple(jax.ShapeDtypeStruct(size, F32) for size in outputs),
        in_specs=[hbm] * 4,
        out_specs=(hbm,) * 4,
        scratch_shapes=[pltpu.VMEM(size, F32) for size in sizes] + [pltpu.SemaphoreType.DMA((8,))],
        compiler_params=pltpu.CompilerParams(vmem_limit_bytes=63 * 2**20),
        name="deliver",
    )(wide, normed, query_grad, loss)
    return loss[0, 0], query_grad, head_grad, bias_grad.reshape(-1)


def solution(mesh):
    return jax.shard_map(
        shards,
        mesh=mesh,
        in_specs=(
            P(("ctx", "cls"), None),
            P(),
            P("cls", "ctx"),
            P("ctx"),
            P("ctx", "cls"),
            P("cls"),
            P("cls"),
        ),
        out_specs=(P(), P("cls", "ctx"), P("ctx", "cls"), P("cls")),
        check_vma=False,
    )
```
